32 devices in a mesh: row: 2 (over core), col: 4 (over z), layer: 4 (over y, x).
Axes of the slice: x: 2, y: 2, z: 4, core: 2. Of those that a mesh axis runs over, the one named last changes fastest.
Arguments:
- panel_top: float32 [4, 1024, 1024], P('layer', 'row', 'col'), as said below
- panel_win: float32 [4, 1024, 1024], P('layer', 'col', 'row'), may hold values from -0.75 to 0.75
- panel_rest: float32 [4, 2688, 1024], P('layer', 'row', 'col'), may hold values from -0.75 to 0.75
- trail_rest: float32 [4, 2688, 1024], P('layer', 'row', 'col'), may hold values from -4 to 4
Outputs:
- factor_top: float32 [1024, 1024], P('row', 'col')
- factor_win: float32 [1024, 1024], P('col', 'row')
- factor_rest: float32 [2688, 1024], P(('row', 'layer'), 'col')
- schur: float32 [2688, 1024], P(('row', 'layer'), 'col')
The draws below stay inside these ranges and needn't reach their ends.
Inputs may be any that keep to these rules, and one draw needn't show every extreme that they name: `panel_top`: each layer's block is symmetric, and the sum over the layers is positive definite with no eigenvalue under 0.25.
All inputs are finite; a program needn't handle non-finite values.
Results may differ from the reference program's by a relative error of at most 0.00021.
Values sent between devices are 32-bit elements; how exact they have to be, the bound alone decides.
A program may use at most 128 MiB of HBM per device.

```python
import jax
import jax.numpy as jnp
from jax import lax

PW = 1024
W = 1024
REST = 2688
N_LAYER = 4


def draw_panel_top(key, part):
    columns_each = max(PW // (2 * N_LAYER), 1)
    base = jax.random.normal(jax.random.fold_in(key, 11), (N_LAYER, PW, columns_each), jnp.float32)
    gram = jnp.einsum('lik,ljk->lij', base, base, precision=lax.Precision.HIGHEST) * (2.75 / PW)
    shift = jax.random.uniform(jax.random.fold_in(key, 12), (N_LAYER, PW), jnp.float32, 0.25, 1.0) / N_LAYER
    identity = jnp.eye(PW, dtype=jnp.float32)
    return gram + shift[:, :, None] * identity[None, :, :]


def with_spikes(values, key, source, target, blocks, factor):
    owner, partner = [(jnp.arange(values.shape[dim]) // (values.shape[dim] // blocks)).reshape([-1 if axis == dim else 1 for axis in range(values.ndim)]) for dim in (source, target)]
    chosen = jax.random.permutation(key, blocks)[partner]
    strong = (owner == chosen) | (owner == (partner + blocks // 2) % blocks)
    return jnp.where(strong, factor * values, values)


def block_levels(rng, dims, cuts, least, high):
    level = 1.0
    for position, parts in cuts:
        steps = jax.random.uniform(jax.random.fold_in(jax.random.fold_in(rng, 6), position), (parts,), jnp.float32, least / len(cuts), high / len(cuts))
        level = level * jnp.repeat(jnp.exp(steps), dims[position] // parts).reshape((-1,) + (1,) * (len(dims) - 1 - position))
    return level


def scatter_about(own_key, dims, spread, reach, pieces=(), held_as=jnp.bfloat16):
    values = spread * jax.random.normal(own_key, dims, jnp.float32)
    if pieces:
        values = values * block_levels(own_key, dims, pieces, -0.22, 0.18)
    return jnp.clip(values, -reach, reach).astype(held_as)


def noise_with(rng, dims, width, limit, split, heavy, kind=jnp.bfloat16):
    array = width * jax.random.normal(rng, dims, jnp.float32)
    if split:
        array = array * block_levels(rng, dims, split, -0.22, 0.18)
    return jnp.clip(with_spikes(array, jax.random.fold_in(rng, 3), *heavy), -limit, limit).astype(kind)


def setup_inputs(seed: int = 0) -> dict:
    keys = jax.random.split(jax.random.key(seed), 5)
    panel_top = draw_panel_top(jax.random.fold_in(keys[4], 71), 0)
    panel_win = scatter_about(keys[1], (N_LAYER, W, PW), (16 * N_LAYER) ** -0.5, 0.75, ((0, 4), (1, 4), (2, 2)), jnp.float32)
    panel_rest = scatter_about(keys[2], (N_LAYER, REST, PW), (16 * N_LAYER) ** -0.5, 0.75, ((0, 4), (1, 2), (2, 4)), jnp.float32)
    trail_rest = noise_with(keys[3], (N_LAYER, REST, W), N_LAYER ** -0.5, 4.0, ((0, 4), (1, 2), (2, 4)), (0, 1, 4, 2.0), jnp.float32)
    return dict(panel_top=panel_top, panel_win=panel_win, panel_rest=panel_rest, trail_rest=trail_rest)


def solve_right(factor, values):
    return jax.scipy.linalg.solve_triangular(factor, values.T, lower=True).T

def reference(panel_top, panel_win, panel_rest, trail_rest):
    top_full = jnp.sum(panel_top, axis=0)
    window = jnp.sum(panel_win, axis=0)
    rest_sum = jnp.sum(panel_rest, axis=0)
    trail = jnp.sum(trail_rest, axis=0)
    factor_top = jnp.linalg.cholesky(top_full)
    factor_win = solve_right(factor_top, window)
    factor_rest = solve_right(factor_top, rest_sum)
    schur = trail - jnp.dot(factor_rest.astype(jnp.float32), factor_win.T.astype(jnp.float32), precision=lax.Precision.HIGHEST, preferred_element_type=jnp.float32)
    return (factor_top, factor_win, factor_rest, schur)
```

```python
import jax
import jax.numpy as jnp
from jax import lax
from jax.experimental import pallas as pl
from jax.experimental.pallas import tpu as pltpu
from jax.sharding import PartitionSpec as P

B = 128
HI = lax.Precision.HIGHEST


def dot(a, b, ca=1, cb=0):
    return lax.dot_general(
        a, b, (((ca,), (cb,)), ((), ())), precision=HI, preferred_element_type=jnp.float32
    )


def factor_block(a):
    n = B // 8
    sub = lax.broadcasted_iota(jnp.int32, (8, B), 0)
    lane = lax.broadcasted_iota(jnp.int32, (8, B), 1)
    left = [a[8 * t : 8 * t + 8, :] for t in range(n)]
    right = [jnp.where(lane == sub + 8 * t, 1.0, 0.0).astype(jnp.float32) for t in range(n)]
    for b in range(n):
        cols = [
            {t: jnp.broadcast_to(left[t][:, 8 * b + j : 8 * b + j + 1], (8, B)) for t in range(b, n)}
            for j in range(8)
        ]
        diag = jnp.zeros((8, B), jnp.float32)
        for i in range(8):
            diag = jnp.where(sub == i, cols[i][b], diag)
            inv = 1.0 / cols[i][b][i : i + 1, :]
            pivots = [cols[l][b][i : i + 1, :] for l in range(8)]
            row_l, row_r = left[b][i : i + 1, :], right[b][i : i + 1, :]
            for t in range(b, n):
                if t == b and i == 7:
                    continue
                m = cols[i][t] * inv
                if t == b:
                    m = jnp.where(sub > i, m, 0.0)
                for l in range(i + 1, 8):
                    cols[l][t] = cols[l][t] - m * pivots[l]
                left[t] = left[t] - m * row_l
                right[t] = right[t] - m * row_r
        scale = lax.rsqrt(diag)
        left[b] = left[b] * scale
        right[b] = right[b] * scale
    return jnp.concatenate(left, 0), jnp.concatenate(right, 0)


def chol_kernel(n_col, g_ref, u_ref, inv_ref, a_ref):
    pieces, rows, cols = g_ref.shape
    size = a_ref.shape[0]
    for p in range(pieces):
        r, c = p // n_col, p % n_col
        a_ref[r * rows : (r + 1) * rows, c * cols : (c + 1) * cols] = g_ref[p]
    blocks = size // B

    def step(k, carry):
        here = pl.ds(pl.multiple_of(k * B, B), B)
        u_diag, inv = factor_block(a_ref[here, here])
        inv_ref[k] = inv
        row = dot(inv, a_ref[here, :])
        at_row = lax.broadcasted_iota(jnp.int32, (B, size), 0) + k * B
        at_col = lax.broadcasted_iota(jnp.int32, (B, size), 1)
        row = jnp.where(at_col >= at_row, row, 0.0)
        u_ref[here, :] = row
        upper = lax.broadcasted_iota(jnp.int32, (B, B), 1) >= lax.broadcasted_iota(
            jnp.int32, (B, B), 0
        )
        u_ref[here, here] = jnp.where(upper, u_diag, 0.0)

        def update(r, carry):
            there = pl.ds(pl.multiple_of(r * B, B), B)
            a_ref[there, :] = a_ref[there, :] - dot(u_ref[here, there], u_ref[here, :], 0, 0)
            return carry

        return lax.fori_loop(k + 1, blocks, update, carry)

    lax.fori_loop(0, blocks, step, 0)


def solve_kernel(win_ref, rest_ref, trail_ref, u_ref, inv_ref, fw_ref, fr_ref, s_ref):
    blocks = inv_ref.shape[0]
    fw_ref[...] = win_ref[...]
    fr_ref[...] = rest_ref[...]
    for j in range(blocks):
        here, after = slice(j * B, (j + 1) * B), slice((j + 1) * B, blocks * B)
        for x_ref in (fw_ref, fr_ref):
            x = dot(x_ref[:, here], inv_ref[j], 1, 1)
            x_ref[:, here] = x
            if j + 1 < blocks:
                x_ref[:, after] = x_ref[:, after] - dot(x, u_ref[here, after])
    s_ref[...] = trail_ref[...] - dot(fr_ref[...], fw_ref[...], 1, 1)


def vmem(n):
    return [pl.BlockSpec(memory_space=pltpu.VMEM)] * n


def per_device(panel_top, panel_win, panel_rest, trail_rest):
    rows_here, cols_here = panel_top.shape[1:]
    n_row, n_col = lax.axis_size("row"), lax.axis_size("col")
    size = rows_here * n_row
    top_part = lax.psum_scatter(panel_top[0], "layer", scatter_dimension=0, tiled=True)
    top_all = lax.all_gather(top_part, ("row", "layer", "col"), axis=0, tiled=False)
    top_all, panel_win, panel_rest, trail_rest = lax.optimization_barrier(
        (top_all, panel_win, panel_rest, trail_rest)
    )
    rest_part = lax.psum_scatter(panel_rest[0], "layer", scatter_dimension=0, tiled=True)
    rest_full = lax.all_gather(rest_part, "col", axis=1, tiled=True)
    win_sum = lax.psum(panel_win[0], "layer")
    window = lax.all_gather(win_sum, "row", axis=1, tiled=True)
    trail = lax.psum_scatter(trail_rest[0], "layer", scatter_dimension=0, tiled=True)

    params = pltpu.CompilerParams(vmem_limit_bytes=40 * 2**20)
    upper, inverses = pl.pallas_call(
        lambda *refs: chol_kernel(n_col, *refs),
        out_shape=(
            jax.ShapeDtypeStruct((size, size), jnp.float32),
            jax.ShapeDtypeStruct((size // B, B, B), jnp.float32),
        ),
        in_specs=vmem(1),
        out_specs=tuple(vmem(2)),
        scratch_shapes=[pltpu.VMEM((size, size), jnp.float32)],
        compiler_params=params,
        cost_estimate=pl.CostEstimate(
            flops=80 * size**3, bytes_accessed=12 * size**2, transcendentals=0
        ),
        name="factor",
    )(top_all)
    factor_win, factor_rest, schur = pl.pallas_call(
        solve_kernel,
        out_shape=(
            jax.ShapeDtypeStruct(window.shape, jnp.float32),
            jax.ShapeDtypeStruct(rest_full.shape, jnp.float32),
            jax.ShapeDtypeStruct(trail.shape, jnp.float32),
        ),
        in_specs=vmem(5),
        out_specs=tuple(vmem(3)),
        compiler_params=params,
        name="solve",
    )(window, rest_full, trail, upper, inverses)

    top_block = lax.dynamic_slice(
        upper,
        (lax.axis_index("col") * cols_here, lax.axis_index("row") * rows_here),
        (cols_here, rows_here),
    ).T
    row_cols = size // n_row
    win_block = lax.dynamic_slice_in_dim(factor_win, lax.axis_index("row") * row_cols, row_cols, 1)
    rest_block = lax.dynamic_slice_in_dim(
        factor_rest, lax.axis_index("col") * cols_here, cols_here, 1
    )
    return (top_block, win_block, rest_block, schur)


def solution(mesh):
    return jax.shard_map(
        per_device,
        mesh=mesh,
        in_specs=(
            P("layer", "row", "col"),
            P("layer", "col", "row"),
            P("layer", "row", "col"),
            P("layer", "row", "col"),
        ),
        out_specs=(
            P("row", "col"),
            P("col", "row"),
            P(("row", "layer"), "col"),
            P(("row", "layer"), "col"),
        ),
        check_vma=False,
    )
```
